32 devices in a mesh: corpus: 8 (over z, x), rep: 4 (over y, core).
Axes of the slice: x: 2, y: 2, z: 4, core: 2. Of those that a mesh axis runs over, the one named last changes fastest.
Arguments:
- queries: bfloat16 [4096, 768], P(('corpus', 'rep')), may hold values from -18 to 18
- teacher: float32 [4096, 64], P(('corpus', 'rep')), may hold values from -15 to 305
- slab: bfloat16 [8192, 768], P('corpus'), may hold values from -12 to 12
- candidates: int32 [4096, 64], P(('corpus', 'rep')), may hold values from 0 to 8191, as said below
- hot_ids: int32 [256], replicated, may hold values from 0 to 8191, as said below
- location: int32 [8192], replicated, may hold values from 0 to 8191, as said below
Outputs:
- loss: float32 [4096], P(('corpus', 'rep'))
- query_grad: float32 [4096, 768], P(('corpus', 'rep'))
- slab_grad: float32 [8192, 768], P(('corpus', 'rep'))
The draws below stay inside these ranges and needn't reach their ends.
Inputs may be any that keep to these rules, and one draw needn't show every extreme that they name: `candidates`: every query names 64 passage ids, exactly 8 of them absent from hot_ids; ids may repeat. With the owner of id p being location[p] // 1024, the ids absent from hot_ids among one device's 128 queries (aligned blocks of 128 rows) fall at most 192 times on any owner; in each block some owner gets exactly 192, the same owner for all blocks whose block number has the same remainder modulo the number of rep devices. `hot_ids`: 256 distinct ids; entries 32 * c to 32 * c + 31 are owned by corpus index c. `location`: A permutation of the passage ids onto slab rows.
All inputs are finite; a program needn't handle non-finite values.
Results may differ from the reference program's by a relative error of at most 0.0026.
Values may be sent and summed in bfloat16 or wider, within the bound.
A program may use at most 128 MiB of HBM per device.

```python
import math
import jax
import jax.numpy as jnp
from jax import lax

D = 768
K = 64
COLD = 8
HOT_DEV = 32
Q_DEV = 128
P_DEV = 1024
H = 256
Q = 4096
P_SIZE = 8192
CAP = 192


def row_scales(key, count, low, high):
    return jnp.exp(jax.random.uniform(key, (count, 1), jnp.float32, math.log(low), math.log(high)))


def layout(key):
    base_key = jax.random.fold_in(key, 7001)
    groups = P_SIZE // P_DEV
    owner_keys = jax.random.split(jax.random.fold_in(base_key, 1), groups)
    owner_perm = jax.vmap(lambda one_key: jax.random.permutation(one_key, P_DEV))(owner_keys).astype(jnp.int32)
    id_of_row = jax.random.permutation(jax.random.fold_in(base_key, 2), P_SIZE).astype(jnp.int32)
    location = jnp.argsort(id_of_row).astype(jnp.int32)
    hot_where = (jnp.arange(groups, dtype=jnp.int32)[:, None] * P_DEV + owner_perm[:, :HOT_DEV]).reshape(H)
    hot_list = id_of_row[hot_where]
    return (owner_perm, id_of_row, location, hot_list)


def draw_location(key, part):
    return layout(key)[2]


def draw_hot_ids(key, part):
    return layout(key)[3]


def draw_candidates(key, part):
    owner_perm, id_of_row, location, hot_list = layout(key)
    groups = P_SIZE // P_DEV
    rep_count = Q // (Q_DEV * groups)
    blocks = Q // Q_DEV
    cold_passage_count = Q_DEV * COLD
    tickets = groups * CAP
    busy = jax.random.randint(jax.random.fold_in(key, 7101), (rep_count,), 0, groups)

    def one_block(block_num):
        blk_key = jax.random.fold_in(jax.random.fold_in(key, 7201), block_num)
        ticket_owner = jnp.arange(tickets, dtype=jnp.int32) // CAP
        order = jax.random.permutation(jax.random.fold_in(blk_key, 1), tickets).astype(jnp.int32)
        priority = order - (ticket_owner == busy[block_num % rep_count]).astype(jnp.int32) * tickets
        chosen = jnp.argsort(priority)[:cold_passage_count]
        owners = ticket_owner[chosen]
        owners = owners[jax.random.permutation(jax.random.fold_in(blk_key, 2), cold_passage_count)]
        pick = jax.random.randint(jax.random.fold_in(blk_key, 3), (cold_passage_count,), HOT_DEV, P_DEV)
        local_rows = owner_perm[owners, pick]
        cold_ids = id_of_row[owners * P_DEV + local_rows]
        hot_pick = jax.random.randint(jax.random.fold_in(blk_key, 4), (Q_DEV * (K - COLD),), 0, H)
        hot_part = hot_list[hot_pick]
        merged = jnp.concatenate([cold_ids.reshape(Q_DEV, COLD), hot_part.reshape(Q_DEV, K - COLD)], axis=1)
        sort_keys = jax.random.randint(jax.random.fold_in(blk_key, 5), (Q_DEV, K), 0, 1 << 20) * K + jnp.arange(K, dtype=jnp.int32)[None, :]
        placing = jnp.argsort(sort_keys, axis=1)
        return jnp.take_along_axis(merged, placing, axis=1)
    return lax.map(one_block, jnp.arange(blocks, dtype=jnp.int32)).reshape(Q, K).astype(jnp.int32)


def draw_queries(key, part):
    spread = row_scales(jax.random.fold_in(key, 101), Q, 0.3, 3.0)
    values = jax.random.truncated_normal(jax.random.fold_in(key, 102), -6.0, 6.0, (Q, D), jnp.float32) * spread
    return values.astype(jnp.bfloat16)


def draw_slab(key, part):
    spread = row_scales(jax.random.fold_in(key, 201), P_SIZE, 0.5, 2.0)
    values = jax.random.truncated_normal(jax.random.fold_in(key, 202), -6.0, 6.0, (P_SIZE, D), jnp.float32) * spread
    return values.astype(jnp.bfloat16)


def draw_teacher(key, part):
    values = 2.5 * jax.random.truncated_normal(jax.random.fold_in(key, 302), -6.0, 6.0, (Q, K), jnp.float32)
    return values


def setup_inputs(seed: int = 0) -> dict:
    streams_of = jax.random.split(jax.random.key(seed), 7)
    return {
        "queries": draw_queries(jax.random.fold_in(streams_of[6], 71), 0),
        "teacher": draw_teacher(jax.random.fold_in(streams_of[6], 71), 0),
        "slab": draw_slab(jax.random.fold_in(streams_of[6], 71), 0),
        "candidates": draw_candidates(jax.random.fold_in(streams_of[6], 71), 0),
        "hot_ids": draw_hot_ids(jax.random.fold_in(streams_of[6], 71), 0),
        "location": draw_location(jax.random.fold_in(streams_of[6], 71), 0),
    }


def distill(student_logits, hot_scores, teacher, cold_mask, hot_index):
    row_top = jnp.maximum(lax.optimization_barrier(jnp.max(student_logits, axis=1)), lax.optimization_barrier(jnp.max(hot_scores, axis=1)))[:, None]
    totals = lax.optimization_barrier(jnp.sum(jnp.exp(student_logits - row_top), axis=1)) + lax.optimization_barrier(jnp.sum(jnp.exp(hot_scores - row_top), axis=1))
    log_partition_total = row_top[:, 0] + jnp.log(totals)
    teach_top = lax.optimization_barrier(jnp.max(teacher, axis=1, keepdims=True))
    shifted = teacher - teach_top
    log_target = shifted - jnp.log(lax.optimization_barrier(jnp.sum(jnp.exp(shifted), axis=1, keepdims=True)))
    target = jnp.exp(log_target)
    loss_rows = lax.optimization_barrier(jnp.sum(target * (log_target - student_logits), axis=1)) + log_partition_total
    d_scores = jnp.exp(student_logits - log_partition_total[:, None]) - target
    d_hot = jnp.exp(hot_scores - log_partition_total[:, None])
    row_index = jnp.broadcast_to(jnp.arange(student_logits.shape[0], dtype=jnp.int32)[:, None], student_logits.shape)
    coef_hot = d_hot.at[row_index, hot_index].add(jnp.where(cold_mask, 0.0, d_scores)).astype(jnp.bfloat16)
    cold_passage_weight = jnp.where(cold_mask, d_scores, 0.0).astype(jnp.bfloat16)
    return (loss_rows, coef_hot, cold_passage_weight)

def reference(queries, teacher, slab, candidates, hot_ids, location):
    logit_scale = 2.0 / math.sqrt(D)
    hot_where = location[hot_ids]
    hot_mark = jnp.full((P_SIZE,), -1, jnp.int32).at[hot_where].set(jnp.arange(H, dtype=jnp.int32))
    hot_emb = slab[hot_where]

    def block_step(carry, block_idx):
        slab_acc, hot_acc = carry
        start = (block_idx * Q_DEV).astype(jnp.int32)
        query_blk = lax.dynamic_slice_in_dim(queries, start, Q_DEV)
        teach_blk = lax.dynamic_slice_in_dim(teacher, start, Q_DEV)
        cand_blk = lax.dynamic_slice_in_dim(candidates, start, Q_DEV)
        slab_rows = location[cand_blk]
        hot_slot = hot_mark[slab_rows]
        cold_mask = hot_slot < 0
        hot_index = jnp.maximum(hot_slot, 0)
        selected_scores = slab[slab_rows].astype(jnp.float32)
        query_broadcast = query_blk.astype(jnp.float32)
        student_logits = logit_scale * jnp.einsum('ho,hao->ha', query_broadcast, selected_scores)
        hot_scores = logit_scale * jnp.dot(query_blk, hot_emb.T, preferred_element_type=jnp.float32)
        loss_rows, coef_hot, cold_passage_weight = distill(student_logits, hot_scores, teach_blk, cold_mask, hot_index)
        cold_score_sum = jnp.einsum('xj,xjz->xz', cold_passage_weight.astype(jnp.float32), selected_scores)
        query_grad = logit_scale * (jnp.dot(coef_hot, hot_emb, preferred_element_type=jnp.float32) + cold_score_sum)
        terms = (logit_scale * cold_passage_weight.astype(jnp.float32)[:, :, None] * query_broadcast[:, None, :]).astype(jnp.bfloat16)
        target_rows = jnp.where(cold_mask, slab_rows, P_SIZE).reshape(-1)
        slab_acc = slab_acc.at[target_rows].add(terms.reshape(-1, D).astype(jnp.float32), mode='drop')
        hot_acc = hot_acc + logit_scale * jnp.dot(coef_hot.T, query_blk, preferred_element_type=jnp.float32)
        return ((slab_acc, hot_acc), (loss_rows, query_grad))
    init = (jnp.zeros((P_SIZE, D), jnp.float32), jnp.zeros((H, D), jnp.float32))
    (slab_acc, hot_acc), (loss_rows, query_grad) = lax.scan(block_step, init, jnp.arange(Q // Q_DEV, dtype=jnp.int32))
    slab_grad = slab_acc.at[hot_where].add(hot_acc)
    return (loss_rows.reshape(Q), query_grad.reshape(Q, D), slab_grad)
```

```python
import math

import jax
import jax.numpy as jnp
from jax import lax
from jax.sharding import PartitionSpec as P

COLD = 8
LANES = 128


def lookup(table, ids):
    rows = table.shape[0] // LANES
    grid = table.reshape(rows, LANES)
    halves = jnp.concatenate([grid // 256, grid % 256], axis=1).astype(jnp.bfloat16)
    pick_row = (ids[:, None] // LANES == jnp.arange(rows, dtype=jnp.int32)[None, :]).astype(
        jnp.bfloat16
    )
    got = jnp.dot(pick_row, halves, preferred_element_type=jnp.float32)
    value = got[:, :LANES] * 256.0 + got[:, LANES:]
    lane = ids[:, None] % LANES == jnp.arange(LANES, dtype=jnp.int32)[None, :]
    return jnp.sum(jnp.where(lane, value, 0.0), axis=1).astype(jnp.int32)


def prepare(teacher, candidates, hot_ids, location):
    q_rows, cand_count = candidates.shape
    teach_top = jnp.max(teacher, axis=1, keepdims=True)
    shifted = teacher - teach_top
    log_target = shifted - jnp.log(jnp.sum(jnp.exp(shifted), axis=1, keepdims=True))
    target = jnp.exp(log_target)
    entropy = jnp.sum(target * log_target, axis=1)
    match = candidates[:, :, None] == hot_ids[None, None, :]
    count = jnp.sum(match.astype(jnp.float32), axis=1)
    target_sum = jnp.sum(jnp.where(match, target[:, :, None], 0.0), axis=1)
    cold = jnp.logical_not(jnp.any(match, axis=2))
    iota = jnp.arange(cand_count, dtype=jnp.int32)
    upto = (iota[:, None] <= iota[None, :]).astype(jnp.bfloat16)
    rank = jnp.dot(cold.astype(jnp.bfloat16), upto, preferred_element_type=jnp.float32)
    slot = jnp.where(cold, rank.astype(jnp.int32) - 1, -1)
    pick = slot[:, None, :] == jnp.arange(COLD, dtype=jnp.int32)[None, :, None]
    cold_ids = jnp.sum(jnp.where(pick, candidates[:, None, :], 0), axis=2)
    cold_target = jnp.sum(jnp.where(pick, target[:, None, :], 0.0), axis=2)
    cold_rows = lookup(location, cold_ids.reshape(-1)).reshape(q_rows, COLD)
    return entropy, count, target_sum, cold_rows, cold_target


def shards(queries, teacher, slab, candidates, hot_ids, location):
    groups = lax.axis_size("corpus")
    reps = lax.axis_size("rep")
    me = lax.axis_index("corpus")
    q_rows, feat_dim = queries.shape
    per_owner = slab.shape[0]
    hot_each = hot_ids.shape[0] // groups
    scale = 2.0 / math.sqrt(feat_dim)
    f32 = jnp.float32

    all_queries = lax.all_gather(queries, "corpus", axis=0, tiled=True)
    entropy, count, target_sum, cold_rows, cold_target = prepare(
        teacher, candidates, hot_ids, location
    )
    parts = [
        count.reshape(q_rows, groups, hot_each).transpose(1, 0, 2),
        target_sum.reshape(q_rows, groups, hot_each).transpose(1, 0, 2),
        jnp.broadcast_to(cold_rows.astype(f32)[None], (groups, q_rows, COLD)),
        jnp.broadcast_to(cold_target[None], (groups, q_rows, COLD)),
    ]
    message = lax.all_to_all(
        jnp.concatenate(parts, axis=2), "corpus", split_axis=0, concat_axis=0, tiled=True
    ).reshape(groups * q_rows, -1)
    count = message[:, :hot_each]
    target_sum = message[:, hot_each : 2 * hot_each]
    cold_rows = message[:, 2 * hot_each : 2 * hot_each + COLD].astype(jnp.int32)
    cold_target = message[:, 2 * hot_each + COLD :]

    own_ids = lax.dynamic_slice_in_dim(hot_ids, me * hot_each, hot_each)
    own_hot = lookup(location, own_ids) - me * per_owner
    row_iota = jnp.arange(per_owner, dtype=jnp.int32)
    place = (own_hot[:, None] == row_iota[None, :]).astype(jnp.bfloat16)
    hot_emb = jnp.dot(place, slab, preferred_element_type=f32).astype(jnp.bfloat16)

    across = (((1,), (1,)), ((), ()))
    hot_scores = scale * lax.dot_general(all_queries, hot_emb, across, preferred_element_type=f32)
    scores = scale * lax.dot_general(all_queries, slab, across, preferred_element_type=f32)
    local = cold_rows - me * per_owner
    mine = (local >= 0) & (local < per_owner)
    cold_scores = jnp.stack(
        [
            jnp.sum(jnp.where(local[:, c, None] == row_iota[None, :], scores, 0.0), axis=1)
            for c in range(COLD)
        ],
        axis=1,
    )
    top = jnp.maximum(
        jnp.max(hot_scores, axis=1), jnp.max(jnp.where(mine, cold_scores, -jnp.inf), axis=1)
    )
    total = jnp.sum((1.0 + count) * jnp.exp(hot_scores - top[:, None]), axis=1) + jnp.sum(
        jnp.where(mine, jnp.exp(cold_scores - top[:, None]), 0.0), axis=1
    )
    dots = jnp.sum(target_sum * hot_scores, axis=1) + jnp.sum(
        jnp.where(mine, cold_target * cold_scores, 0.0), axis=1
    )
    stats = lax.all_gather(jnp.stack([top, total, dots]), "corpus", axis=0)
    tops = stats[:, 0]
    row_top = jnp.max(tops, axis=0)
    log_total = row_top + jnp.log(jnp.sum(stats[:, 1] * jnp.exp(tops - row_top[None]), axis=0))
    loss_all = log_total - jnp.sum(stats[:, 2], axis=0)
    loss_rows = entropy + lax.dynamic_slice_in_dim(loss_all, me * q_rows, q_rows)

    hot_weight = (
        (1.0 + count) * jnp.exp(hot_scores - log_total[:, None]) - target_sum
    ).astype(jnp.bfloat16)
    cold_weight = jnp.where(mine, jnp.exp(cold_scores - log_total[:, None]) - cold_target, 0.0)
    cold_weight = cold_weight.astype(jnp.bfloat16).astype(f32)
    weight = jnp.dot(hot_weight, place, preferred_element_type=f32)
    for c in range(COLD):
        weight = weight + jnp.where(
            local[:, c, None] == row_iota[None, :], cold_weight[:, c, None], 0.0
        )
    weight = weight.astype(jnp.bfloat16)

    slab_part = scale * lax.dot_general(
        weight, all_queries, (((0,), (0,)), ((), ())), preferred_element_type=f32
    )
    slab_parts = lax.all_to_all(
        slab_part.astype(jnp.bfloat16).reshape(reps, per_owner // reps, feat_dim),
        "rep", split_axis=0, concat_axis=0, tiled=True,
    )
    query_part = scale * jnp.dot(weight, slab, preferred_element_type=f32)
    query_parts = lax.all_to_all(
        query_part.astype(jnp.bfloat16).reshape(groups, q_rows, feat_dim),
        "corpus", split_axis=0, concat_axis=0, tiled=True,
    )
    slab_grad = jnp.sum(slab_parts.astype(f32), axis=0)
    query_grad = jnp.sum(query_parts.astype(f32), axis=0)
    return (loss_rows, query_grad, slab_grad)


def solution(mesh):
    return jax.shard_map(
        shards,
        mesh=mesh,
        in_specs=(
            P(("corpus", "rep"), None),
            P(("corpus", "rep"), None),
            P("corpus", None),
            P(("corpus", "rep"), None),
            P(),
            P(),
        ),
        out_specs=(P(("corpus", "rep")), P(("corpus", "rep"), None), P(("corpus", "rep"), None)),
        check_vma=False,
    )
```

```python
import math

import jax
import jax.numpy as jnp
from jax import lax
from jax.sharding import PartitionSpec as P

COLD = 8
LANES = 128


def lookup(table, ids):
    rows = table.shape[0] // LANES
    grid = table.reshape(rows, LANES)
    halves = jnp.concatenate([grid // 256, grid % 256], axis=1).astype(jnp.bfloat16)
    pick_row = (ids[:, None] // LANES == jnp.arange(rows, dtype=jnp.int32)[None, :]).astype(
        jnp.bfloat16
    )
    got = jnp.dot(pick_row, halves, preferred_element_type=jnp.float32)
    value = got[:, :LANES] * 256.0 + got[:, LANES:]
    lane = ids[:, None] % LANES == jnp.arange(LANES, dtype=jnp.int32)[None, :]
    return jnp.sum(jnp.where(lane, value, 0.0), axis=1).astype(jnp.int32)


def prepare(teacher, candidates, hot_ids, location):
    q_rows, cand_count = candidates.shape
    teach_top = jnp.max(teacher, axis=1, keepdims=True)
    shifted = teacher - teach_top
    log_target = shifted - jnp.log(jnp.sum(jnp.exp(shifted), axis=1, keepdims=True))
    target = jnp.exp(log_target)
    entropy = jnp.sum(target * log_target, axis=1)
    match = candidates[:, :, None] == hot_ids[None, None, :]
    count = jnp.sum(match.astype(jnp.float32), axis=1)
    target_sum = jnp.sum(jnp.where(match, target[:, :, None], 0.0), axis=1)
    cold = jnp.logical_not(jnp.any(match, axis=2))
    iota = jnp.arange(cand_count, dtype=jnp.int32)
    upto = (iota[:, None] <= iota[None, :]).astype(jnp.bfloat16)
    rank = jnp.dot(cold.astype(jnp.bfloat16), upto, preferred_element_type=jnp.float32)
    slot = jnp.where(cold, rank.astype(jnp.int32) - 1, -1)
    pick = slot[:, None, :] == jnp.arange(COLD, dtype=jnp.int32)[None, :, None]
    cold_ids = jnp.sum(jnp.where(pick, candidates[:, None, :], 0), axis=2)
    cold_target = jnp.sum(jnp.where(pick, target[:, None, :], 0.0), axis=2)
    cold_rows = lookup(location, cold_ids.reshape(-1)).reshape(q_rows, COLD)
    return entropy, count, target_sum, cold_rows, cold_target


def shards(queries, teacher, slab, candidates, hot_ids, location):
    groups = lax.axis_size("corpus")
    reps = lax.axis_size("rep")
    me = lax.axis_index("corpus")
    q_rows, feat_dim = queries.shape
    per_owner = slab.shape[0]
    hot_each = hot_ids.shape[0] // groups
    scale = 2.0 / math.sqrt(feat_dim)
    f32 = jnp.float32

    all_queries = lax.all_gather(queries, "corpus", axis=0, tiled=True)
    entropy, count, target_sum, cold_rows, cold_target = prepare(
        teacher, candidates, hot_ids, location
    )
    parts = [
        count.reshape(q_rows, groups, hot_each).transpose(1, 0, 2),
        target_sum.reshape(q_rows, groups, hot_each).transpose(1, 0, 2),
        jnp.broadcast_to(cold_rows.astype(f32)[None], (groups, q_rows, COLD)),
        jnp.broadcast_to(cold_target[None], (groups, q_rows, COLD)),
    ]
    message = lax.all_to_all(
        jnp.concatenate(parts, axis=2), "corpus", split_axis=0, concat_axis=0, tiled=True
    ).reshape(groups * q_rows, -1)
    count = message[:, :hot_each]
    target_sum = message[:, hot_each : 2 * hot_each]
    cold_rows = message[:, 2 * hot_each : 2 * hot_each + COLD].astype(jnp.int32)
    cold_target = message[:, 2 * hot_each + COLD :]

    own_ids = lax.dynamic_slice_in_dim(hot_ids, me * hot_each, hot_each)
    own_hot = lookup(location, own_ids) - me * per_owner
    row_iota = jnp.arange(per_owner, dtype=jnp.int32)
    place = (own_hot[:, None] == row_iota[None, :]).astype(jnp.bfloat16)
    hot_emb = jnp.dot(place, slab, preferred_element_type=f32).astype(jnp.bfloat16)

    across = (((1,), (1,)), ((), ()))
    hot_scores = scale * lax.dot_general(all_queries, hot_emb, across, preferred_element_type=f32)
    scores = scale * lax.dot_general(all_queries, slab, across, preferred_element_type=f32)
    local = cold_rows - me * per_owner
    mine = (local >= 0) & (local < per_owner)
    cold_scores = jnp.stack(
        [
            jnp.sum(jnp.where(local[:, c, None] == row_iota[None, :], scores, 0.0), axis=1)
            for c in range(COLD)
        ],
        axis=1,
    )
    top = jnp.maximum(
        jnp.max(hot_scores, axis=1), jnp.max(jnp.where(mine, cold_scores, -jnp.inf), axis=1)
    )
    total = jnp.sum((1.0 + count) * jnp.exp(hot_scores - top[:, None]), axis=1) + jnp.sum(
        jnp.where(mine, jnp.exp(cold_scores - top[:, None]), 0.0), axis=1
    )
    dots = jnp.sum(target_sum * hot_scores, axis=1) + jnp.sum(
        jnp.where(mine, cold_target * cold_scores, 0.0), axis=1
    )
    stats = jnp.stack([top, total, dots])
    stats = lax.all_to_all(
        jnp.broadcast_to(stats[None], (groups, *stats.shape)),
        "corpus", split_axis=0, concat_axis=0, tiled=True,
    )
    tops = stats[:, 0]
    row_top = jnp.max(tops, axis=0)
    log_total = row_top + jnp.log(jnp.sum(stats[:, 1] * jnp.exp(tops - row_top[None]), axis=0))
    loss_all = log_total - jnp.sum(stats[:, 2], axis=0)
    loss_rows = entropy + lax.dynamic_slice_in_dim(loss_all, me * q_rows, q_rows)

    hot_weight = (
        (1.0 + count) * jnp.exp(hot_scores - log_total[:, None]) - target_sum
    ).astype(jnp.bfloat16)
    cold_weight = jnp.where(mine, jnp.exp(cold_scores - log_total[:, None]) - cold_target, 0.0)
    cold_weight = cold_weight.astype(jnp.bfloat16).astype(f32)
    weight = jnp.dot(hot_weight, place, preferred_element_type=f32)
    for c in range(COLD):
        weight = weight + jnp.where(
            local[:, c, None] == row_iota[None, :], cold_weight[:, c, None], 0.0
        )
    weight = weight.astype(jnp.bfloat16)

    query_part = scale * jnp.dot(weight, slab, preferred_element_type=f32)
    query_parts = lax.all_to_all(
        query_part.astype(jnp.bfloat16).reshape(groups, q_rows, feat_dim),
        "corpus", split_axis=0, concat_axis=0, tiled=True,
    )
    slab_part = scale * lax.dot_general(
        weight, all_queries, (((0,), (0,)), ((), ())), preferred_element_type=f32
    )
    slab_part = slab_part.astype(jnp.bfloat16).reshape(reps, per_owner // reps, feat_dim)
    rep = lax.axis_index("rep")
    slab_grad = lax.dynamic_index_in_dim(slab_part, rep, 0, keepdims=False).astype(f32)
    for step in range(1, reps):
        outgoing = lax.dynamic_index_in_dim(slab_part, (rep + step) % reps, 0, keepdims=False)
        arrived = lax.ppermute(outgoing, "rep", [(r, (r + step) % reps) for r in range(reps)])
        slab_grad = slab_grad + arrived.astype(f32)
    query_grad = jnp.sum(query_parts.astype(f32), axis=0)
    return (loss_rows, query_grad, slab_grad)


def solution(mesh):
    return jax.shard_map(
        shards,
        mesh=mesh,
        in_specs=(
            P(("corpus", "rep"), None),
            P(("corpus", "rep"), None),
            P("corpus", None),
            P(("corpus", "rep"), None),
            P(),
            P(),
        ),
        out_specs=(P(("corpus", "rep")), P(("corpus", "rep"), None), P(("corpus", "rep"), None)),
        check_vma=False,
    )
```

```python
import math

import jax
import jax.numpy as jnp
from jax import lax
from jax.sharding import PartitionSpec as P

COLD = 8
LANES = 128


def lookup(table, ids):
    rows = table.shape[0] // LANES
    grid = table.reshape(rows, LANES)
    halves = jnp.concatenate([grid // 256, grid % 256], axis=1).astype(jnp.bfloat16)
    pick_row = (ids[:, None] // LANES == jnp.arange(rows, dtype=jnp.int32)[None, :]).astype(
        jnp.bfloat16
    )
    got = jnp.dot(pick_row, halves, preferred_element_type=jnp.float32)
    value = got[:, :LANES] * 256.0 + got[:, LANES:]
    lane = ids[:, None] % LANES == jnp.arange(LANES, dtype=jnp.int32)[None, :]
    return jnp.sum(jnp.where(lane, value, 0.0), axis=1).astype(jnp.int32)


def prepare(teacher, candidates, hot_ids, location):
    q_rows, cand_count = candidates.shape
    teach_top = jnp.max(teacher, axis=1, keepdims=True)
    shifted = teacher - teach_top
    log_target = shifted - jnp.log(jnp.sum(jnp.exp(shifted), axis=1, keepdims=True))
    target = jnp.exp(log_target)
    entropy = jnp.sum(target * log_target, axis=1)
    match = candidates[:, :, None] == hot_ids[None, None, :]
    count = jnp.sum(match.astype(jnp.float32), axis=1)
    target_sum = jnp.sum(jnp.where(match, target[:, :, None], 0.0), axis=1)
    cold = jnp.logical_not(jnp.any(match, axis=2))
    iota = jnp.arange(cand_count, dtype=jnp.int32)
    upto = (iota[:, None] <= iota[None, :]).astype(jnp.bfloat16)
    rank = jnp.dot(cold.astype(jnp.bfloat16), upto, preferred_element_type=jnp.float32)
    slot = jnp.where(cold, rank.astype(jnp.int32) - 1, -1)
    pick = slot[:, None, :] == jnp.arange(COLD, dtype=jnp.int32)[None, :, None]
    cold_ids = jnp.sum(jnp.where(pick, candidates[:, None, :], 0), axis=2)
    cold_target = jnp.sum(jnp.where(pick, target[:, None, :], 0.0), axis=2)
    cold_rows = lookup(location, cold_ids.reshape(-1)).reshape(q_rows, COLD)
    return entropy, count, target_sum, cold_rows, cold_target


def gather_blocks(block, axis):
    groups = lax.axis_size(axis)
    if groups & (groups - 1):
        return lax.all_gather(block, axis, axis=0)
    me = lax.axis_index(axis)
    held = block[None]
    bit = groups // 2
    while bit:
        other = lax.ppermute(held, axis, [(i, i ^ bit) for i in range(groups)])
        upper = (me // bit) % 2 == 1
        first = jnp.where(upper, other, held)
        second = jnp.where(upper, held, other)
        held = jnp.stack([first, second], axis=1).reshape(-1, *block.shape)
        bit //= 2
    return held


def score(all_queries, message, slab, hot_emb, base, hot_each, scale):
    f32 = jnp.float32
    per_owner = slab.shape[0]
    row_iota = jnp.arange(per_owner, dtype=jnp.int32)
    count = message[:, :hot_each]
    target_sum = message[:, hot_each : 2 * hot_each]
    cold_rows = message[:, 2 * hot_each : 2 * hot_each + COLD].astype(jnp.int32)
    cold_target = message[:, 2 * hot_each + COLD :]
    across = (((1,), (1,)), ((), ()))
    hot_scores = scale * lax.dot_general(all_queries, hot_emb, across, preferred_element_type=f32)
    scores = scale * lax.dot_general(all_queries, slab, across, preferred_element_type=f32)
    local = cold_rows - base
    mine = (local >= 0) & (local < per_owner)
    cold_scores = jnp.stack(
        [
            jnp.sum(jnp.where(local[:, c, None] == row_iota[None, :], scores, 0.0), axis=1)
            for c in range(COLD)
        ],
        axis=1,
    )
    top = jnp.maximum(
        jnp.max(hot_scores, axis=1), jnp.max(jnp.where(mine, cold_scores, -jnp.inf), axis=1)
    )
    total = jnp.sum((1.0 + count) * jnp.exp(hot_scores - top[:, None]), axis=1) + jnp.sum(
        jnp.where(mine, jnp.exp(cold_scores - top[:, None]), 0.0), axis=1
    )
    dots = jnp.sum(target_sum * hot_scores, axis=1) + jnp.sum(
        jnp.where(mine, cold_target * cold_scores, 0.0), axis=1
    )
    stats = jnp.stack([top, total, dots])
    return stats, (hot_scores, count, target_sum, local, mine, cold_scores, cold_target)


def weigh(kept, log_total, place):
    hot_scores, count, target_sum, local, mine, cold_scores, cold_target = kept
    f32 = jnp.float32
    row_iota = jnp.arange(place.shape[1], dtype=jnp.int32)
    hot_weight = (
        (1.0 + count) * jnp.exp(hot_scores - log_total[:, None]) - target_sum
    ).astype(jnp.bfloat16)
    cold_weight = jnp.where(mine, jnp.exp(cold_scores - log_total[:, None]) - cold_target, 0.0)
    cold_weight = cold_weight.astype(jnp.bfloat16).astype(f32)
    weight = jnp.dot(hot_weight, place, preferred_element_type=f32)
    for c in range(COLD):
        weight = weight + jnp.where(
            local[:, c, None] == row_iota[None, :], cold_weight[:, c, None], 0.0
        )
    return weight.astype(jnp.bfloat16)


def shards(queries, teacher, slab, candidates, hot_ids, location):
    groups = lax.axis_size("corpus")
    reps = lax.axis_size("rep")
    me = lax.axis_index("corpus")
    q_rows, feat_dim = queries.shape
    per_owner = slab.shape[0]
    hot_each = hot_ids.shape[0] // groups
    scale = 2.0 / math.sqrt(feat_dim)
    f32 = jnp.float32

    half = q_rows // 2
    all_queries = [gather_blocks(queries[:half], "corpus"), gather_blocks(queries[half:], "corpus")]
    entropy, count, target_sum, cold_rows, cold_target = prepare(
        teacher, candidates, hot_ids, location
    )
    parts = [
        count.reshape(q_rows, groups, hot_each).transpose(1, 0, 2),
        target_sum.reshape(q_rows, groups, hot_each).transpose(1, 0, 2),
        jnp.broadcast_to(cold_rows.astype(f32)[None], (groups, q_rows, COLD)),
        jnp.broadcast_to(cold_target[None], (groups, q_rows, COLD)),
    ]
    message = lax.all_to_all(
        jnp.concatenate(parts, axis=2), "corpus", split_axis=0, concat_axis=0, tiled=True
    )

    own_ids = lax.dynamic_slice_in_dim(hot_ids, me * hot_each, hot_each)
    own_hot = lookup(location, own_ids) - me * per_owner
    row_iota = jnp.arange(per_owner, dtype=jnp.int32)
    place = (own_hot[:, None] == row_iota[None, :]).astype(jnp.bfloat16)
    hot_emb = jnp.dot(place, slab, preferred_element_type=f32).astype(jnp.bfloat16)

    queries_of = [part.reshape(-1, feat_dim) for part in all_queries]
    messages = [message[:, :half], message[:, half:]]
    stats, kept = [], []
    for part, text in zip(queries_of, messages):
        one, rest = score(
            part, text.reshape(part.shape[0], -1), slab, hot_emb, me * per_owner, hot_each, scale
        )
        stats.append(one)
        kept.append(rest)
    stats = jnp.concatenate(stats, axis=1)
    stats = lax.all_to_all(
        jnp.broadcast_to(stats[None], (groups, *stats.shape)),
        "corpus", split_axis=0, concat_axis=0, tiled=True,
    )
    tops = stats[:, 0]
    row_top = jnp.max(tops, axis=0)
    log_total = row_top + jnp.log(jnp.sum(stats[:, 1] * jnp.exp(tops - row_top[None]), axis=0))
    loss_all = log_total - jnp.sum(stats[:, 2], axis=0)
    split = groups * half
    loss_own = [
        lax.dynamic_slice_in_dim(loss_all[:split], me * half, half),
        lax.dynamic_slice_in_dim(loss_all[split:], me * (q_rows - half), q_rows - half),
    ]
    loss_rows = entropy + jnp.concatenate(loss_own)

    weights = [
        weigh(kept[0], log_total[:split], place),
        weigh(kept[1], log_total[split:], place),
    ]
    query_part = jnp.concatenate(
        [
            (scale * jnp.dot(weight, slab, preferred_element_type=f32))
            .astype(jnp.bfloat16)
            .reshape(groups, -1, feat_dim)
            for weight in weights
        ],
        axis=1,
    )
    query_parts = lax.all_to_all(
        query_part, "corpus", split_axis=0, concat_axis=0, tiled=True
    )
    down = (((0,), (0,)), ((), ()))
    slab_part = scale * sum(
        lax.dot_general(weight, part, down, preferred_element_type=f32)
        for weight, part in zip(weights, queries_of)
    )
    slab_part = slab_part.astype(jnp.bfloat16).reshape(reps, per_owner // reps, feat_dim)
    rep = lax.axis_index("rep")
    slab_grad = lax.dynamic_index_in_dim(slab_part, rep, 0, keepdims=False).astype(f32)
    for step in range(1, reps):
        outgoing = lax.dynamic_index_in_dim(slab_part, (rep + step) % reps, 0, keepdims=False)
        arrived = lax.ppermute(outgoing, "rep", [(r, (r + step) % reps) for r in range(reps)])
        slab_grad = slab_grad + arrived.astype(f32)
    query_grad = jnp.sum(query_parts.astype(f32), axis=0)
    return (loss_rows, query_grad, slab_grad)


def solution(mesh):
    return jax.shard_map(
        shards,
        mesh=mesh,
        in_specs=(
            P(("corpus", "rep"), None),
            P(("corpus", "rep"), None),
            P("corpus", None),
            P(("corpus", "rep"), None),
            P(),
            P(),
        ),
        out_specs=(P(("corpus", "rep")), P(("corpus", "rep"), None), P(("corpus", "rep"), None)),
        check_vma=False,
    )
```

```python
import math

import jax
import jax.numpy as jnp
from jax import lax
from jax.sharding import PartitionSpec as P

COLD = 8
LANES = 128


def lookup(table, ids):
    rows = table.shape[0] // LANES
    grid = table.reshape(rows, LANES)
    halves = jnp.concatenate([grid // 256, grid % 256], axis=1).astype(jnp.bfloat16)
    pick_row = (ids[:, None] // LANES == jnp.arange(rows, dtype=jnp.int32)[None, :]).astype(
        jnp.bfloat16
    )
    got = jnp.dot(pick_row, halves, preferred_element_type=jnp.float32)
    value = got[:, :LANES] * 256.0 + got[:, LANES:]
    lane = ids[:, None] % LANES == jnp.arange(LANES, dtype=jnp.int32)[None, :]
    return jnp.sum(jnp.where(lane, value, 0.0), axis=1).astype(jnp.int32)


def prepare(teacher, candidates, hot_ids, location):
    q_rows, cand_count = candidates.shape
    teach_top = jnp.max(teacher, axis=1, keepdims=True)
    shifted = teacher - teach_top
    log_target = shifted - jnp.log(jnp.sum(jnp.exp(shifted), axis=1, keepdims=True))
    target = jnp.exp(log_target)
    entropy = jnp.sum(target * log_target, axis=1)
    match = candidates[:, :, None] == hot_ids[None, None, :]
    count = jnp.sum(match.astype(jnp.float32), axis=1)
    target_sum = jnp.sum(jnp.where(match, target[:, :, None], 0.0), axis=1)
    cold = jnp.logical_not(jnp.any(match, axis=2))
    iota = jnp.arange(cand_count, dtype=jnp.int32)
    upto = (iota[:, None] <= iota[None, :]).astype(jnp.bfloat16)
    rank = jnp.dot(cold.astype(jnp.bfloat16), upto, preferred_element_type=jnp.float32)
    slot = jnp.where(cold, rank.astype(jnp.int32) - 1, -1)
    pick = slot[:, None, :] == jnp.arange(COLD, dtype=jnp.int32)[None, :, None]
    cold_ids = jnp.sum(jnp.where(pick, candidates[:, None, :], 0), axis=2)
    cold_target = jnp.sum(jnp.where(pick, target[:, None, :], 0.0), axis=2)
    cold_rows = lookup(location, cold_ids.reshape(-1)).reshape(q_rows, COLD)
    return entropy, count, target_sum, cold_rows, cold_target


def in_order(blocks, index):
    bit = 1
    while bit < len(blocks):
        swap = (index // bit) % 2 == 1
        blocks = [jnp.where(swap, blocks[i ^ bit], blocks[i]) for i in range(len(blocks))]
        bit *= 2
    return blocks


def by_pairs(groups):
    return 4 <= groups <= 16 and groups & (groups - 1) == 0


def swap_with(block, distance, groups):
    return lax.ppermute(block, "corpus", [(i, i ^ distance) for i in range(groups)])


def shards(queries, teacher, slab, candidates, hot_ids, location):
    groups = lax.axis_size("corpus")
    reps = lax.axis_size("rep")
    me = lax.axis_index("corpus")
    q_rows, feat_dim = queries.shape
    per_owner = slab.shape[0]
    hot_each = hot_ids.shape[0] // groups
    scale = 2.0 / math.sqrt(feat_dim)
    f32 = jnp.float32

    if by_pairs(groups):
        far = [swap_with(queries, 2 * d, groups) for d in range(groups // 2 - 1, 0, -1)][::-1]
        near = swap_with(queries, 1, groups)
    entropy, count, target_sum, cold_rows, cold_target = prepare(
        teacher, candidates, hot_ids, location
    )
    parts = [
        count.reshape(q_rows, groups, hot_each).transpose(1, 0, 2),
        target_sum.reshape(q_rows, groups, hot_each).transpose(1, 0, 2),
        jnp.broadcast_to(cold_rows.astype(f32)[None], (groups, q_rows, COLD)),
        jnp.broadcast_to(cold_target[None], (groups, q_rows, COLD)),
    ]
    message = jnp.concatenate(parts, axis=2)
    if by_pairs(groups):
        message, far = lax.optimization_barrier((message, far))
        passed = swap_with(jnp.stack(far), 1, groups)
        upper = me % 2 == 1
        mine_all = [queries, *far]
        others = [near, *[passed[d] for d in range(len(far))]]
        lower_half = [jnp.where(upper, o, m) for m, o in zip(mine_all, others)]
        upper_half = [jnp.where(upper, m, o) for m, o in zip(mine_all, others)]
        lower_half = in_order(lower_half, me // 2)
        upper_half = in_order(upper_half, me // 2)
        all_queries = jnp.concatenate([b for pair in zip(lower_half, upper_half) for b in pair])
    else:
        all_queries = lax.all_gather(queries, "corpus", axis=0, tiled=True)
    message = lax.all_to_all(
        message, "corpus", split_axis=0, concat_axis=0, tiled=True
    ).reshape(groups * q_rows, -1)
    count = message[:, :hot_each]
    target_sum = message[:, hot_each : 2 * hot_each]
    cold_rows = message[:, 2 * hot_each : 2 * hot_each + COLD].astype(jnp.int32)
    cold_target = message[:, 2 * hot_each + COLD :]

    own_ids = lax.dynamic_slice_in_dim(hot_ids, me * hot_each, hot_each)
    own_hot = lookup(location, own_ids) - me * per_owner
    row_iota = jnp.arange(per_owner, dtype=jnp.int32)
    place = (own_hot[:, None] == row_iota[None, :]).astype(jnp.bfloat16)
    hot_emb = jnp.dot(place, slab, preferred_element_type=f32).astype(jnp.bfloat16)

    across = (((1,), (1,)), ((), ()))
    hot_scores = scale * lax.dot_general(all_queries, hot_emb, across, preferred_element_type=f32)
    scores = scale * lax.dot_general(all_queries, slab, across, preferred_element_type=f32)
    local = cold_rows - me * per_owner
    mine = (local >= 0) & (local < per_owner)
    cold_scores = jnp.stack(
        [
            jnp.sum(jnp.where(local[:, c, None] == row_iota[None, :], scores, 0.0), axis=1)
            for c in range(COLD)
        ],
        axis=1,
    )
    top = jnp.maximum(
        jnp.max(hot_scores, axis=1), jnp.max(jnp.where(mine, cold_scores, -jnp.inf), axis=1)
    )
    total = jnp.sum((1.0 + count) * jnp.exp(hot_scores - top[:, None]), axis=1) + jnp.sum(
        jnp.where(mine, jnp.exp(cold_scores - top[:, None]), 0.0), axis=1
    )
    dots = jnp.sum(target_sum * hot_scores, axis=1) + jnp.sum(
        jnp.where(mine, cold_target * cold_scores, 0.0), axis=1
    )
    stats = jnp.stack([top, total, dots])
    stats = lax.all_to_all(
        jnp.broadcast_to(stats[None], (groups, *stats.shape)),
        "corpus", split_axis=0, concat_axis=0, tiled=True,
    )
    tops = stats[:, 0]
    row_top = jnp.max(tops, axis=0)
    log_total = row_top + jnp.log(jnp.sum(stats[:, 1] * jnp.exp(tops - row_top[None]), axis=0))
    loss_all = log_total - jnp.sum(stats[:, 2], axis=0)
    loss_rows = entropy + lax.dynamic_slice_in_dim(loss_all, me * q_rows, q_rows)

    hot_weight = (
        (1.0 + count) * jnp.exp(hot_scores - log_total[:, None]) - target_sum
    ).astype(jnp.bfloat16)
    cold_weight = jnp.where(mine, jnp.exp(cold_scores - log_total[:, None]) - cold_target, 0.0)
    cold_weight = cold_weight.astype(jnp.bfloat16).astype(f32)
    weight = jnp.dot(hot_weight, place, preferred_element_type=f32)
    for c in range(COLD):
        weight = weight + jnp.where(
            local[:, c, None] == row_iota[None, :], cold_weight[:, c, None], 0.0
        )
    weight = weight.astype(jnp.bfloat16)

    query_part = scale * jnp.dot(weight, slab, preferred_element_type=f32)
    query_parts = lax.all_to_all(
        query_part.astype(jnp.bfloat16).reshape(groups, q_rows, feat_dim),
        "corpus", split_axis=0, concat_axis=0, tiled=True,
    )
    slab_part = scale * lax.dot_general(
        weight, all_queries, (((0,), (0,)), ((), ())), preferred_element_type=f32
    )
    slab_part = slab_part.astype(jnp.bfloat16).reshape(reps, per_owner // reps, feat_dim)
    rep = lax.axis_index("rep")
    slab_grad = lax.dynamic_index_in_dim(slab_part, rep, 0, keepdims=False).astype(f32)
    for step in range(1, reps):
        outgoing = lax.dynamic_index_in_dim(slab_part, (rep + step) % reps, 0, keepdims=False)
        arrived = lax.ppermute(outgoing, "rep", [(r, (r + step) % reps) for r in range(reps)])
        slab_grad = slab_grad + arrived.astype(f32)
    query_grad = jnp.sum(query_parts.astype(f32), axis=0)
    return (loss_rows, query_grad, slab_grad)


def solution(mesh):
    return jax.shard_map(
        shards,
        mesh=mesh,
        in_specs=(
            P(("corpus", "rep"), None),
            P(("corpus", "rep"), None),
            P("corpus", None),
            P(("corpus", "rep"), None),
            P(),
            P(),
        ),
        out_specs=(P(("corpus", "rep")), P(("corpus", "rep"), None), P(("corpus", "rep"), None)),
        check_vma=False,
    )
```

```python
import math

import jax
import jax.numpy as jnp
from jax import lax
from jax.sharding import PartitionSpec as P

COLD = 8
LANES = 128


def lookup(table, ids):
    rows = table.shape[0] // LANES
    grid = table.reshape(rows, LANES)
    halves = jnp.concatenate([grid // 256, grid % 256], axis=1).astype(jnp.bfloat16)
    pick_row = (ids[:, None] // LANES == jnp.arange(rows, dtype=jnp.int32)[None, :]).astype(
        jnp.bfloat16
    )
    got = jnp.dot(pick_row, halves, preferred_element_type=jnp.float32)
    value = got[:, :LANES] * 256.0 + got[:, LANES:]
    lane = ids[:, None] % LANES == jnp.arange(LANES, dtype=jnp.int32)[None, :]
    return jnp.sum(jnp.where(lane, value, 0.0), axis=1).astype(jnp.int32)


def prepare(teacher, candidates, hot_ids, location):
    q_rows, cand_count = candidates.shape
    teach_top = jnp.max(teacher, axis=1, keepdims=True)
    shifted = teacher - teach_top
    log_target = shifted - jnp.log(jnp.sum(jnp.exp(shifted), axis=1, keepdims=True))
    target = jnp.exp(log_target)
    entropy = jnp.sum(target * log_target, axis=1)
    match = candidates[:, :, None] == hot_ids[None, None, :]
    count = jnp.sum(match.astype(jnp.float32), axis=1)
    target_sum = jnp.sum(jnp.where(match, target[:, :, None], 0.0), axis=1)
    cold = jnp.logical_not(jnp.any(match, axis=2))
    iota = jnp.arange(cand_count, dtype=jnp.int32)
    upto = (iota[:, None] <= iota[None, :]).astype(jnp.bfloat16)
    rank = jnp.dot(cold.astype(jnp.bfloat16), upto, preferred_element_type=jnp.float32)
    slot = jnp.where(cold, rank.astype(jnp.int32) - 1, -1)
    pick = slot[:, None, :] == jnp.arange(COLD, dtype=jnp.int32)[None, :, None]
    cold_ids = jnp.sum(jnp.where(pick, candidates[:, None, :], 0), axis=2)
    cold_target = jnp.sum(jnp.where(pick, target[:, None, :], 0.0), axis=2)
    cold_rows = lookup(location, cold_ids.reshape(-1)).reshape(q_rows, COLD)
    return entropy, count, target_sum, cold_rows, cold_target


def in_order(blocks, index):
    bit = 1
    while bit < len(blocks):
        swap = (index // bit) % 2 == 1
        blocks = [jnp.where(swap, blocks[i ^ bit], blocks[i]) for i in range(len(blocks))]
        bit *= 2
    return blocks


def by_pairs(groups):
    return 4 <= groups <= 16 and groups & (groups - 1) == 0


def swap_with(block, distance, groups):
    return lax.ppermute(block, "corpus", [(i, i ^ distance) for i in range(groups)])


def shards(queries, teacher, slab, candidates, hot_ids, location):
    groups = lax.axis_size("corpus")
    reps = lax.axis_size("rep")
    me = lax.axis_index("corpus")
    q_rows, feat_dim = queries.shape
    per_owner = slab.shape[0]
    hot_each = hot_ids.shape[0] // groups
    scale = 2.0 / math.sqrt(feat_dim)
    f32 = jnp.float32

    if by_pairs(groups):
        far = [swap_with(queries, 2 * d, groups) for d in range(groups // 2 - 1, 0, -1)][::-1]
        near = swap_with(queries, 1, groups)
    entropy, count, target_sum, cold_rows, cold_target = prepare(
        teacher, candidates, hot_ids, location
    )
    parts = [
        count.reshape(q_rows, groups, hot_each).transpose(1, 0, 2),
        target_sum.reshape(q_rows, groups, hot_each).transpose(1, 0, 2),
        jnp.broadcast_to(cold_rows.astype(f32)[None], (groups, q_rows, COLD)),
        jnp.broadcast_to(cold_target[None], (groups, q_rows, COLD)),
    ]
    message = jnp.concatenate(parts, axis=2)
    if by_pairs(groups):
        message, far = lax.optimization_barrier((message, far))
        passed = swap_with(jnp.stack(far), 1, groups)
        upper = me % 2 == 1
        mine_all = [queries, *far]
        others = [near, *[passed[d] for d in range(len(far))]]
        lower_half = [jnp.where(upper, o, m) for m, o in zip(mine_all, others)]
        upper_half = [jnp.where(upper, m, o) for m, o in zip(mine_all, others)]
        lower_half = in_order(lower_half, me // 2)
        upper_half = in_order(upper_half, me // 2)
        all_queries = jnp.concatenate([b for pair in zip(lower_half, upper_half) for b in pair])
    else:
        all_queries = lax.all_gather(queries, "corpus", axis=0, tiled=True)
    message = lax.all_to_all(
        message, "corpus", split_axis=0, concat_axis=0, tiled=True
    ).reshape(groups * q_rows, -1)
    count = message[:, :hot_each]
    target_sum = message[:, hot_each : 2 * hot_each]
    cold_rows = message[:, 2 * hot_each : 2 * hot_each + COLD].astype(jnp.int32)
    cold_target = message[:, 2 * hot_each + COLD :]

    own_ids = lax.dynamic_slice_in_dim(hot_ids, me * hot_each, hot_each)
    own_hot = lookup(location, own_ids) - me * per_owner
    row_iota = jnp.arange(per_owner, dtype=jnp.int32)
    place = (own_hot[:, None] == row_iota[None, :]).astype(jnp.bfloat16)
    hot_emb = jnp.dot(place, slab, preferred_element_type=f32).astype(jnp.bfloat16)

    across = (((1,), (1,)), ((), ()))
    hot_scores = scale * lax.dot_general(all_queries, hot_emb, across, preferred_element_type=f32)
    scores = scale * lax.dot_general(all_queries, slab, across, preferred_element_type=f32)
    local = cold_rows - me * per_owner
    mine = (local >= 0) & (local < per_owner)
    cold_scores = jnp.stack(
        [
            jnp.sum(jnp.where(local[:, c, None] == row_iota[None, :], scores, 0.0), axis=1)
            for c in range(COLD)
        ],
        axis=1,
    )
    top = jnp.maximum(
        jnp.max(hot_scores, axis=1), jnp.max(jnp.where(mine, cold_scores, -jnp.inf), axis=1)
    )
    total = jnp.sum((1.0 + count) * jnp.exp(hot_scores - top[:, None]), axis=1) + jnp.sum(
        jnp.where(mine, jnp.exp(cold_scores - top[:, None]), 0.0), axis=1
    )
    dots = jnp.sum(target_sum * hot_scores, axis=1) + jnp.sum(
        jnp.where(mine, cold_target * cold_scores, 0.0), axis=1
    )
    stats = jnp.stack([top, total, dots])
    stats = lax.all_to_all(
        jnp.broadcast_to(stats[None], (groups, *stats.shape)),
        "corpus", split_axis=0, concat_axis=0, tiled=True,
    )
    tops = stats[:, 0]
    row_top = jnp.max(tops, axis=0)
    log_total = row_top + jnp.log(jnp.sum(stats[:, 1] * jnp.exp(tops - row_top[None]), axis=0))
    loss_all = log_total - jnp.sum(stats[:, 2], axis=0)
    loss_rows = entropy + lax.dynamic_slice_in_dim(loss_all, me * q_rows, q_rows)

    hot_weight = (
        (1.0 + count) * jnp.exp(hot_scores - log_total[:, None]) - target_sum
    ).astype(jnp.bfloat16)
    cold_weight = jnp.where(mine, jnp.exp(cold_scores - log_total[:, None]) - cold_target, 0.0)
    cold_weight = cold_weight.astype(jnp.bfloat16).astype(f32)
    weight = jnp.dot(hot_weight, place, preferred_element_type=f32)
    for c in range(COLD):
        weight = weight + jnp.where(
            local[:, c, None] == row_iota[None, :], cold_weight[:, c, None], 0.0
        )
    weight = weight.astype(jnp.bfloat16)

    query_part = scale * jnp.dot(weight, slab, preferred_element_type=f32)
    if by_pairs(groups):
        query_part = query_part.reshape(groups // 2, 2, q_rows, feat_dim)
        give, keep = query_part[:, 0], query_part[:, 1]
        upper = me % 2 == 1
        give, keep = jnp.where(upper, give, keep), jnp.where(upper, keep, give)
        give = give.astype(jnp.bfloat16)
        query_grad = None
        halfway = []
        for d in range(groups // 2 - 1, -1, -1):
            target = (me // 2) ^ d
            block = lax.dynamic_index_in_dim(give, target, 0, keepdims=False)
            halfway.append((d, target, swap_with(block, 1, groups)))
        far_parts = []
        for d, target, arrived in halfway:
            both = lax.dynamic_index_in_dim(keep, target, 0, keepdims=False) + arrived.astype(f32)
            if d:
                far_parts.append(swap_with(both.astype(jnp.bfloat16), 2 * d, groups))
            else:
                query_grad = both
        for part in far_parts:
            query_grad = query_grad + part.astype(f32)
    else:
        query_parts = lax.all_to_all(
            query_part.astype(jnp.bfloat16).reshape(groups, q_rows, feat_dim),
            "corpus", split_axis=0, concat_axis=0, tiled=True,
        )
        query_grad = jnp.sum(query_parts.astype(f32), axis=0)
    slab_part = scale * lax.dot_general(
        weight, all_queries, (((0,), (0,)), ((), ())), preferred_element_type=f32
    )
    slab_part = slab_part.astype(jnp.bfloat16).reshape(reps, per_owner // reps, feat_dim)
    rep = lax.axis_index("rep")
    slab_grad = lax.dynamic_index_in_dim(slab_part, rep, 0, keepdims=False).astype(f32)
    for step in range(1, reps):
        outgoing = lax.dynamic_index_in_dim(slab_part, (rep + step) % reps, 0, keepdims=False)
        arrived = lax.ppermute(outgoing, "rep", [(r, (r + step) % reps) for r in range(reps)])
        slab_grad = slab_grad + arrived.astype(f32)
    return (loss_rows, query_grad, slab_grad)


def solution(mesh):
    return jax.shard_map(
        shards,
        mesh=mesh,
        in_specs=(
            P(("corpus", "rep"), None),
            P(("corpus", "rep"), None),
            P("corpus", None),
            P(("corpus", "rep"), None),
            P(),
            P(),
        ),
        out_specs=(P(("corpus", "rep")), P(("corpus", "rep"), None), P(("corpus", "rep"), None)),
        check_vma=False,
    )
```

```python
import math

import jax
import jax.numpy as jnp
from jax import lax
from jax.sharding import PartitionSpec as P

COLD = 8
LANES = 128


def lookup(table, ids):
    rows = table.shape[0] // LANES
    grid = table.reshape(rows, LANES)
    halves = jnp.concatenate([grid // 256, grid % 256], axis=1).astype(jnp.bfloat16)
    pick_row = (ids[:, None] // LANES == jnp.arange(rows, dtype=jnp.int32)[None, :]).astype(
        jnp.bfloat16
    )
    got = jnp.dot(pick_row, halves, preferred_element_type=jnp.float32)
    value = got[:, :LANES] * 256.0 + got[:, LANES:]
    lane = ids[:, None] % LANES == jnp.arange(LANES, dtype=jnp.int32)[None, :]
    return jnp.sum(jnp.where(lane, value, 0.0), axis=1).astype(jnp.int32)


def prepare(teacher, candidates, hot_ids, location):
    q_rows, cand_count = candidates.shape
    teach_top = jnp.max(teacher, axis=1, keepdims=True)
    shifted = teacher - teach_top
    log_target = shifted - jnp.log(jnp.sum(jnp.exp(shifted), axis=1, keepdims=True))
    target = jnp.exp(log_target)
    entropy = jnp.sum(target * log_target, axis=1)
    match = candidates[:, :, None] == hot_ids[None, None, :]
    count = jnp.sum(match.astype(jnp.float32), axis=1)
    target_sum = jnp.sum(jnp.where(match, target[:, :, None], 0.0), axis=1)
    cold = jnp.logical_not(jnp.any(match, axis=2))
    iota = jnp.arange(cand_count, dtype=jnp.int32)
    upto = (iota[:, None] <= iota[None, :]).astype(jnp.bfloat16)
    rank = jnp.dot(cold.astype(jnp.bfloat16), upto, preferred_element_type=jnp.float32)
    slot = jnp.where(cold, rank.astype(jnp.int32) - 1, -1)
    pick = slot[:, None, :] == jnp.arange(COLD, dtype=jnp.int32)[None, :, None]
    cold_ids = jnp.sum(jnp.where(pick, candidates[:, None, :], 0), axis=2)
    cold_target = jnp.sum(jnp.where(pick, target[:, None, :], 0.0), axis=2)
    cold_rows = lookup(location, cold_ids.reshape(-1)).reshape(q_rows, COLD)
    return entropy, count, target_sum, cold_rows, cold_target


def in_order(blocks, index):
    bit = 1
    while bit < len(blocks):
        swap = (index // bit) % 2 == 1
        blocks = [jnp.where(swap, blocks[i ^ bit], blocks[i]) for i in range(len(blocks))]
        bit *= 2
    return blocks


def by_pairs(groups):
    return 4 <= groups <= 16 and groups & (groups - 1) == 0


def swap_with(block, distance, groups):
    return lax.ppermute(block, "corpus", [(i, i ^ distance) for i in range(groups)])


def shards(queries, teacher, slab, candidates, hot_ids, location):
    groups = lax.axis_size("corpus")
    reps = lax.axis_size("rep")
    me = lax.axis_index("corpus")
    q_rows, feat_dim = queries.shape
    per_owner = slab.shape[0]
    hot_each = hot_ids.shape[0] // groups
    scale = 2.0 / math.sqrt(feat_dim)
    f32 = jnp.float32

    if by_pairs(groups):
        far = [swap_with(queries, 2 * d, groups) for d in range(groups // 2 - 1, 0, -1)][::-1]
        near = swap_with(queries, 1, groups)
    entropy, count, target_sum, cold_rows, cold_target = prepare(
        teacher, candidates, hot_ids, location
    )
    parts = [
        count.reshape(q_rows, groups, hot_each).transpose(1, 0, 2),
        target_sum.reshape(q_rows, groups, hot_each).transpose(1, 0, 2),
        jnp.broadcast_to(cold_rows.astype(f32)[None], (groups, q_rows, COLD)),
        jnp.broadcast_to(cold_target[None], (groups, q_rows, COLD)),
    ]
    message = jnp.concatenate(parts, axis=2)
    if by_pairs(groups):
        message, far = lax.optimization_barrier((message, far))
        passed = swap_with(jnp.stack(far), 1, groups)
        upper = me % 2 == 1
        mine_all = [queries, *far]
        others = [near, *[passed[d] for d in range(len(far))]]
        lower_half = [jnp.where(upper, o, m) for m, o in zip(mine_all, others)]
        upper_half = [jnp.where(upper, m, o) for m, o in zip(mine_all, others)]
        lower_half = in_order(lower_half, me // 2)
        upper_half = in_order(upper_half, me // 2)
        all_queries = jnp.concatenate([b for pair in zip(lower_half, upper_half) for b in pair])
    else:
        all_queries = lax.all_gather(queries, "corpus", axis=0, tiled=True)
    message = lax.all_to_all(
        message, "corpus", split_axis=0, concat_axis=0, tiled=True
    ).reshape(groups * q_rows, -1)
    count = message[:, :hot_each]
    target_sum = message[:, hot_each : 2 * hot_each]
    cold_rows = message[:, 2 * hot_each : 2 * hot_each + COLD].astype(jnp.int32)
    cold_target = message[:, 2 * hot_each + COLD :]

    own_ids = lax.dynamic_slice_in_dim(hot_ids, me * hot_each, hot_each)
    own_hot = lookup(location, own_ids) - me * per_owner
    row_iota = jnp.arange(per_owner, dtype=jnp.int32)
    place = (own_hot[:, None] == row_iota[None, :]).astype(jnp.bfloat16)
    hot_emb = jnp.dot(place, slab, preferred_element_type=f32).astype(jnp.bfloat16)

    across = (((1,), (1,)), ((), ()))
    hot_scores = scale * lax.dot_general(all_queries, hot_emb, across, preferred_element_type=f32)
    scores = scale * lax.dot_general(all_queries, slab, across, preferred_element_type=f32)
    local = cold_rows - me * per_owner
    mine = (local >= 0) & (local < per_owner)
    cold_scores = jnp.stack(
        [
            jnp.sum(jnp.where(local[:, c, None] == row_iota[None, :], scores, 0.0), axis=1)
            for c in range(COLD)
        ],
        axis=1,
    )
    top = jnp.maximum(
        jnp.max(hot_scores, axis=1), jnp.max(jnp.where(mine, cold_scores, -jnp.inf), axis=1)
    )
    total = jnp.sum((1.0 + count) * jnp.exp(hot_scores - top[:, None]), axis=1) + jnp.sum(
        jnp.where(mine, jnp.exp(cold_scores - top[:, None]), 0.0), axis=1
    )
    dots = jnp.sum(target_sum * hot_scores, axis=1) + jnp.sum(
        jnp.where(mine, cold_target * cold_scores, 0.0), axis=1
    )
    stats = jnp.stack([top, total, dots])
    stats = lax.all_to_all(
        jnp.broadcast_to(stats[None], (groups, *stats.shape)),
        "corpus", split_axis=0, concat_axis=0, tiled=True,
    )
    tops = stats[:, 0]
    row_top = jnp.max(tops, axis=0)
    log_total = row_top + jnp.log(jnp.sum(stats[:, 1] * jnp.exp(tops - row_top[None]), axis=0))
    loss_all = log_total - jnp.sum(stats[:, 2], axis=0)
    loss_rows = entropy + lax.dynamic_slice_in_dim(loss_all, me * q_rows, q_rows)

    hot_weight = (
        (1.0 + count) * jnp.exp(hot_scores - log_total[:, None]) - target_sum
    ).astype(jnp.bfloat16)
    cold_weight = jnp.where(mine, jnp.exp(cold_scores - log_total[:, None]) - cold_target, 0.0)
    cold_weight = cold_weight.astype(jnp.bfloat16).astype(f32)
    weight = jnp.dot(hot_weight, place, preferred_element_type=f32)
    for c in range(COLD):
        weight = weight + jnp.where(
            local[:, c, None] == row_iota[None, :], cold_weight[:, c, None], 0.0
        )
    weight = weight.astype(jnp.bfloat16)

    query_part = scale * jnp.dot(weight, slab, preferred_element_type=f32)
    if by_pairs(groups):
        query_part = query_part.reshape(groups // 2, 2, q_rows, feat_dim)
        give, keep = query_part[:, 0], query_part[:, 1]
        upper = me % 2 == 1
        give, keep = jnp.where(upper, give, keep), jnp.where(upper, keep, give)
        give = give.astype(jnp.bfloat16)
        query_grad = None
        halfway = []
        for d in range(groups // 2 - 1, -1, -1):
            target = (me // 2) ^ d
            block = lax.dynamic_index_in_dim(give, target, 0, keepdims=False)
            halfway.append((d, target, swap_with(block, 1, groups)))
        d, target, arrived = halfway[0]
        weight, arrived = lax.optimization_barrier((weight, arrived))
        halfway[0] = (d, target, arrived)
        far_parts = []
        for d, target, arrived in halfway:
            both = lax.dynamic_index_in_dim(keep, target, 0, keepdims=False) + arrived.astype(f32)
            if d:
                far_parts.append(swap_with(both.astype(jnp.bfloat16), 2 * d, groups))
            else:
                query_grad = both
        for part in far_parts:
            query_grad = query_grad + part.astype(f32)
    else:
        query_parts = lax.all_to_all(
            query_part.astype(jnp.bfloat16).reshape(groups, q_rows, feat_dim),
            "corpus", split_axis=0, concat_axis=0, tiled=True,
        )
        query_grad = jnp.sum(query_parts.astype(f32), axis=0)
    slab_part = scale * lax.dot_general(
        weight, all_queries, (((0,), (0,)), ((), ())), preferred_element_type=f32
    )
    slab_part = slab_part.astype(jnp.bfloat16).reshape(reps, per_owner // reps, feat_dim)
    rep = lax.axis_index("rep")
    slab_grad = lax.dynamic_index_in_dim(slab_part, rep, 0, keepdims=False).astype(f32)
    for step in range(1, reps):
        outgoing = lax.dynamic_index_in_dim(slab_part, (rep + step) % reps, 0, keepdims=False)
        arrived = lax.ppermute(outgoing, "rep", [(r, (r + step) % reps) for r in range(reps)])
        slab_grad = slab_grad + arrived.astype(f32)
    return (loss_rows, query_grad, slab_grad)


def solution(mesh):
    return jax.shard_map(
        shards,
        mesh=mesh,
        in_specs=(
            P(("corpus", "rep"), None),
            P(("corpus", "rep"), None),
            P("corpus", None),
            P(("corpus", "rep"), None),
            P(),
            P(),
        ),
        out_specs=(P(("corpus", "rep")), P(("corpus", "rep"), None), P(("corpus", "rep"), None)),
        check_vma=False,
    )
```

```python
import math

import jax
import jax.numpy as jnp
from jax import lax
from jax.sharding import PartitionSpec as P

COLD = 8
LANES = 128


def lookup(table, ids):
    rows = table.shape[0] // LANES
    grid = table.reshape(rows, LANES)
    halves = jnp.concatenate([grid // 256, grid % 256], axis=1).astype(jnp.bfloat16)
    pick_row = (ids[:, None] // LANES == jnp.arange(rows, dtype=jnp.int32)[None, :]).astype(
        jnp.bfloat16
    )
    got = jnp.dot(pick_row, halves, preferred_element_type=jnp.float32)
    value = got[:, :LANES] * 256.0 + got[:, LANES:]
    lane = ids[:, None] % LANES == jnp.arange(LANES, dtype=jnp.int32)[None, :]
    return jnp.sum(jnp.where(lane, value, 0.0), axis=1).astype(jnp.int32)


def prepare(teacher, candidates, hot_ids, location):
    q_rows, cand_count = candidates.shape
    teach_top = jnp.max(teacher, axis=1, keepdims=True)
    shifted = teacher - teach_top
    log_target = shifted - jnp.log(jnp.sum(jnp.exp(shifted), axis=1, keepdims=True))
    target = jnp.exp(log_target)
    entropy = jnp.sum(target * log_target, axis=1)
    match = candidates[:, :, None] == hot_ids[None, None, :]
    count = jnp.sum(match.astype(jnp.float32), axis=1)
    target_sum = jnp.sum(jnp.where(match, target[:, :, None], 0.0), axis=1)
    cold = jnp.logical_not(jnp.any(match, axis=2))
    iota = jnp.arange(cand_count, dtype=jnp.int32)
    upto = (iota[:, None] <= iota[None, :]).astype(jnp.bfloat16)
    rank = jnp.dot(cold.astype(jnp.bfloat16), upto, preferred_element_type=jnp.float32)
    slot = jnp.where(cold, rank.astype(jnp.int32) - 1, -1)
    pick = slot[:, None, :] == jnp.arange(COLD, dtype=jnp.int32)[None, :, None]
    cold_ids = jnp.sum(jnp.where(pick, candidates[:, None, :], 0), axis=2)
    cold_target = jnp.sum(jnp.where(pick, target[:, None, :], 0.0), axis=2)
    cold_rows = lookup(location, cold_ids.reshape(-1)).reshape(q_rows, COLD)
    return entropy, count, target_sum, cold_rows, cold_target


def in_order(blocks, index):
    bit = 1
    while bit < len(blocks):
        swap = (index // bit) % 2 == 1
        blocks = [jnp.where(swap, blocks[i ^ bit], blocks[i]) for i in range(len(blocks))]
        bit *= 2
    return blocks


def by_pairs(groups):
    return 4 <= groups <= 16 and groups & (groups - 1) == 0


def swap_with(block, distance, groups):
    return lax.ppermute(block, "corpus", [(i, i ^ distance) for i in range(groups)])


def shards(queries, teacher, slab, candidates, hot_ids, location):
    groups = lax.axis_size("corpus")
    reps = lax.axis_size("rep")
    me = lax.axis_index("corpus")
    q_rows, feat_dim = queries.shape
    per_owner = slab.shape[0]
    hot_each = hot_ids.shape[0] // groups
    scale = 2.0 / math.sqrt(feat_dim)
    f32 = jnp.float32

    if by_pairs(groups):
        far = [swap_with(queries, 2 * d, groups) for d in range(groups // 2 - 1, 0, -1)][::-1]
        near = swap_with(queries, 1, groups)
    entropy, count, target_sum, cold_rows, cold_target = prepare(
        teacher, candidates, hot_ids, location
    )
    parts = [
        count.reshape(q_rows, groups, hot_each).transpose(1, 0, 2),
        target_sum.reshape(q_rows, groups, hot_each).transpose(1, 0, 2),
        jnp.broadcast_to(cold_rows.astype(f32)[None], (groups, q_rows, COLD)),
        jnp.broadcast_to(cold_target[None], (groups, q_rows, COLD)),
    ]
    message = jnp.concatenate(parts, axis=2)
    if by_pairs(groups):
        message, far = lax.optimization_barrier((message, far))
        passed = swap_with(jnp.stack(far), 1, groups)
        upper = me % 2 == 1
        mine_all = [queries, *far]
        others = [near, *[passed[d] for d in range(len(far))]]
        lower_half = [jnp.where(upper, o, m) for m, o in zip(mine_all, others)]
        upper_half = [jnp.where(upper, m, o) for m, o in zip(mine_all, others)]
        lower_half = in_order(lower_half, me // 2)
        upper_half = in_order(upper_half, me // 2)
        all_queries = jnp.concatenate([b for pair in zip(lower_half, upper_half) for b in pair])
    else:
        all_queries = lax.all_gather(queries, "corpus", axis=0, tiled=True)
    message = lax.all_to_all(
        message, "corpus", split_axis=0, concat_axis=0, tiled=True
    ).reshape(groups * q_rows, -1)
    count = message[:, :hot_each]
    target_sum = message[:, hot_each : 2 * hot_each]
    cold_rows = message[:, 2 * hot_each : 2 * hot_each + COLD].astype(jnp.int32)
    cold_target = message[:, 2 * hot_each + COLD :]

    own_ids = lax.dynamic_slice_in_dim(hot_ids, me * hot_each, hot_each)
    own_hot = lookup(location, own_ids) - me * per_owner
    row_iota = jnp.arange(per_owner, dtype=jnp.int32)
    place = (own_hot[:, None] == row_iota[None, :]).astype(jnp.bfloat16)
    hot_emb = jnp.dot(place, slab, preferred_element_type=f32).astype(jnp.bfloat16)

    across = (((1,), (1,)), ((), ()))
    hot_scores = scale * lax.dot_general(all_queries, hot_emb, across, preferred_element_type=f32)
    scores = scale * lax.dot_general(all_queries, slab, across, preferred_element_type=f32)
    local = cold_rows - me * per_owner
    mine = (local >= 0) & (local < per_owner)
    cold_scores = jnp.stack(
        [
            jnp.sum(jnp.where(local[:, c, None] == row_iota[None, :], scores, 0.0), axis=1)
            for c in range(COLD)
        ],
        axis=1,
    )
    top = jnp.maximum(
        jnp.max(hot_scores, axis=1), jnp.max(jnp.where(mine, cold_scores, -jnp.inf), axis=1)
    )
    total = jnp.sum((1.0 + count) * jnp.exp(hot_scores - top[:, None]), axis=1) + jnp.sum(
        jnp.where(mine, jnp.exp(cold_scores - top[:, None]), 0.0), axis=1
    )
    dots = jnp.sum(target_sum * hot_scores, axis=1) + jnp.sum(
        jnp.where(mine, cold_target * cold_scores, 0.0), axis=1
    )
    stats = jnp.stack([top, total, dots])
    stats = lax.all_to_all(
        jnp.broadcast_to(stats[None], (groups, *stats.shape)),
        "corpus", split_axis=0, concat_axis=0, tiled=True,
    )
    tops = stats[:, 0]
    row_top = jnp.max(tops, axis=0)
    log_total = row_top + jnp.log(jnp.sum(stats[:, 1] * jnp.exp(tops - row_top[None]), axis=0))
    loss_all = log_total - jnp.sum(stats[:, 2], axis=0)
    loss_rows = entropy + lax.dynamic_slice_in_dim(loss_all, me * q_rows, q_rows)

    hot_weight = (
        (1.0 + count) * jnp.exp(hot_scores - log_total[:, None]) - target_sum
    ).astype(jnp.bfloat16)
    cold_weight = jnp.where(mine, jnp.exp(cold_scores - log_total[:, None]) - cold_target, 0.0)
    cold_weight = cold_weight.astype(jnp.bfloat16).astype(f32)
    weight = jnp.dot(hot_weight, place, preferred_element_type=f32)
    for c in range(COLD):
        weight = weight + jnp.where(
            local[:, c, None] == row_iota[None, :], cold_weight[:, c, None], 0.0
        )
    weight = weight.astype(jnp.bfloat16)

    query_part = scale * jnp.dot(weight, slab, preferred_element_type=f32)
    if by_pairs(groups):
        query_part = query_part.reshape(groups // 2, 2, q_rows, feat_dim)
        give, keep = query_part[:, 0], query_part[:, 1]
        upper = me % 2 == 1
        give, keep = jnp.where(upper, give, keep), jnp.where(upper, keep, give)
        give = give.astype(jnp.bfloat16)
        query_grad = None
        halfway = []
        for d in range(groups // 2 - 1, -1, -2):
            targets = [(me // 2) ^ d, (me // 2) ^ (d - 1)]
            pair = jnp.stack(
                [lax.dynamic_index_in_dim(give, t, 0, keepdims=False) for t in targets]
            )
            arrived = swap_with(pair, 1, groups)
            halfway += [(d - n, targets[n], arrived[n]) for n in range(2)]
        far_parts = []
        for d, target, arrived in halfway:
            both = lax.dynamic_index_in_dim(keep, target, 0, keepdims=False) + arrived.astype(f32)
            if d:
                far_parts.append(swap_with(both.astype(jnp.bfloat16), 2 * d, groups))
            else:
                query_grad = both
        for part in far_parts:
            query_grad = query_grad + part.astype(f32)
    else:
        query_parts = lax.all_to_all(
            query_part.astype(jnp.bfloat16).reshape(groups, q_rows, feat_dim),
            "corpus", split_axis=0, concat_axis=0, tiled=True,
        )
        query_grad = jnp.sum(query_parts.astype(f32), axis=0)
    slab_part = scale * lax.dot_general(
        weight, all_queries, (((0,), (0,)), ((), ())), preferred_element_type=f32
    )
    slab_part = slab_part.astype(jnp.bfloat16).reshape(reps, per_owner // reps, feat_dim)
    rep = lax.axis_index("rep")
    slab_grad = lax.dynamic_index_in_dim(slab_part, rep, 0, keepdims=False).astype(f32)
    for step in range(1, reps):
        outgoing = lax.dynamic_index_in_dim(slab_part, (rep + step) % reps, 0, keepdims=False)
        arrived = lax.ppermute(outgoing, "rep", [(r, (r + step) % reps) for r in range(reps)])
        slab_grad = slab_grad + arrived.astype(f32)
    return (loss_rows, query_grad, slab_grad)


def solution(mesh):
    return jax.shard_map(
        shards,
        mesh=mesh,
        in_specs=(
            P(("corpus", "rep"), None),
            P(("corpus", "rep"), None),
            P("corpus", None),
            P(("corpus", "rep"), None),
            P(),
            P(),
        ),
        out_specs=(P(("corpus", "rep")), P(("corpus", "rep"), None), P(("corpus", "rep"), None)),
        check_vma=False,
    )
```
